32 devices in a mesh: seq: 16 (over z, y, x), exp: 2 (over core).
Axes of the slice: x: 2, y: 2, z: 4, core: 2. Of those that a mesh axis runs over, the one named last changes fastest.
Arguments:
- query_input: bfloat16 [2048, 2048], P('seq', 'exp'), may hold values from -4.5 to 4.5
- key_input: bfloat16 [2048, 2048], P('seq', 'exp'), may hold values from -4.5 to 4.5
- value_input: bfloat16 [2048, 2048], P('seq', 'exp'), may hold values from -6 to 6
- segment_ids: int32 [2048], P('seq'), may hold values from 0 to 15, never falling along the last dimension, each value on 1 to 256 neighbouring positions
- residual_in: bfloat16 [2048, 4096], P('seq', 'exp'), may hold values from -13.5 to 13.5
- out_weight: bfloat16 [2048, 4096], P('exp'), may hold values from -0.1875 to 0.1875
- norm_gain: float32 [4096], P('exp'), may hold values from 0.1 to 1.9
- router: bfloat16 [4096, 32], P(None, 'seq'), may hold values from -0.1875 to 0.1875
- modality: int32 [2048], P('seq'), may hold values from 0 to 1
- expert_in: int32 [2048], P('seq'), may hold values from 0 to 15, as said below
- gate_weight: bfloat16 [32, 4096, 2816], P('seq', None, 'exp'), may hold values from -0.09375 to 0.09375
- up_weight: bfloat16 [32, 4096, 2816], P('seq', None, 'exp'), may hold values from -0.09375 to 0.09375
- down_weight: bfloat16 [32, 2816, 4096], P('seq', 'exp'), may hold values from -0.15625 to 0.15625
Outputs:
- layer_out: bfloat16 [2048, 4096], P('seq', 'exp')
The draws below stay inside these ranges and needn't reach their ends.
Inputs may be any that keep to these rules, and one draw needn't show every extreme that they name: `segment_ids`: document numbers never fall along the sequence, and a document holds at most an eighth of the 2048 tokens. `expert_in`: within each aligned block of 128 tokens no expert (modality and number together) is chosen by more than 7 tokens, and in every block some expert is chosen by exactly 7.
All inputs are finite; a program needn't handle non-finite values.
Results may differ from the reference program's by a relative error of at most 0.0095.
Values may be sent and summed in bfloat16 or wider, within the bound.
No kernel may reach another device: no remote copies, remote signals or barrier semaphores. Data moves between devices by JAX's collectives and lax.ppermute only.
A program may use at most 128 MiB of HBM per device.

```python
import math
import jax
import jax.numpy as jnp
import numpy as np
from jax import lax

D = 4096
FF = 2816
HEADS = 16
HEAD_DIM = 128
EXPERTS = 32
DOCS = 16
TOK = 128
MODAL_EXPERTS = 16
SEQ_LEN = 2048
CAPACITY = 7
FF_DEV = 1408
N_SEQ = 16
N_EXP = 2


def routing_choice(key):
    base_key = jax.random.fold_in(key, 101)
    pick_key, count_key, jitter_key, order_key = jax.random.split(base_key, 4)
    block_count = SEQ_LEN // TOK
    hot_experts = jax.random.permutation(pick_key, EXPERTS)[:3]
    is_hot = jnp.zeros((EXPERTS,), jnp.int32).at[hot_experts].set(1)
    lowest = (TOK - 3 * CAPACITY + EXPERTS - 4) // (EXPERTS - 3)
    slot_counts = jax.random.randint(count_key, (block_count, EXPERTS), lowest, CAPACITY)
    slot_counts = jnp.where(is_hot[None, :] == 1, CAPACITY, slot_counts)
    rank_grid = jnp.arange(CAPACITY, dtype=jnp.int32)
    usable = rank_grid[None, None, :] < slot_counts[:, :, None]
    priority = jnp.where(usable, 1 + is_hot[None, :, None], 0)
    jitter = jax.random.randint(jitter_key, (block_count, EXPERTS, CAPACITY), 0, 1024)
    flat_index = jnp.arange(EXPERTS * CAPACITY, dtype=jnp.int32).reshape(EXPERTS, CAPACITY)
    scores = priority * (1 << 25) + jitter * (EXPERTS * CAPACITY) + flat_index[None]
    scores = scores.reshape(block_count, EXPERTS * CAPACITY).astype(jnp.int32)
    ignored_values, chosen = lax.top_k(scores, TOK)
    picked = (chosen // CAPACITY).astype(jnp.int32)
    order_keys = jax.random.split(order_key, block_count)
    shuffled = jax.vmap(jax.random.permutation)(order_keys, picked)
    return shuffled.reshape(SEQ_LEN).astype(jnp.int32)


def draw_modality(key, part):
    return (routing_choice(key) // MODAL_EXPERTS).astype(jnp.int32)


def draw_expert_in(key, part):
    return (routing_choice(key) % MODAL_EXPERTS).astype(jnp.int32)


def drawn_pairs(key):
    base_key = jax.random.fold_in(key, 202)
    query_key, key_key = jax.random.split(base_key, 2)
    columns = HEADS * HEAD_DIM
    query_draw = jnp.clip(jax.random.normal(query_key, (SEQ_LEN, columns), jnp.float32), -4.5, 4.5)
    key_draw = jnp.clip(jax.random.normal(key_key, (SEQ_LEN, columns), jnp.float32), -4.5, 4.5)
    return (query_draw, key_draw)


def draw_query_input(key, part):
    return drawn_pairs(key)[0].astype(jnp.bfloat16)


def draw_key_input(key, part):
    return drawn_pairs(key)[1].astype(jnp.bfloat16)


def draw_residual_in(key, part):
    base_key = jax.random.fold_in(key, 303)
    value_key = jax.random.fold_in(base_key, 0)
    column_ramp = jnp.arange(D, dtype=jnp.float32) / D
    entries = jnp.clip(jax.random.normal(value_key, (SEQ_LEN, D), jnp.float32), -3.0, 3.0) * 0.7 * (3.0 ** column_ramp)[None, :]
    return entries.astype(jnp.bfloat16)


def raised(values, key, source, target, parts, factor):
    def block_of(position):
        return (jnp.arange(values.shape[position]) // (values.shape[position] // parts)).reshape((-1,) + (1,) * (values.ndim - 1 - position))

    first = jax.random.permutation(key, parts)[block_of(target)]
    far = (block_of(target) + parts // 2) % parts
    return jnp.where((block_of(source) == first) | (block_of(source) == far), factor * values, values)


def level_of(key, extent, cuts, low, top_value):
    loudness, own = 1.0, jax.random.fold_in(key, 6)
    for dim, shards_of in cuts:
        draws = jnp.exp(jax.random.uniform(jax.random.fold_in(own, dim), (shards_of,), jnp.float32, low / len(cuts), top_value / len(cuts)))
        loudness = loudness * jnp.repeat(draws, extent[dim] // shards_of).reshape([-1 if axis == dim else 1 for axis in range(len(extent))])
    return loudness


def length_profile(number_of, total, most, slope):
    portions = [(1 << 20) // math.isqrt(rank ** slope) + 1 for rank in range(2, number_of + 1)]
    rest, counts = total - most - (number_of - 1), [1] * (number_of - 1)
    while rest > 0:
        movable = [i for i in range(number_of - 1) if counts[i] < most]
        whole, remaining = sum([portions[i] for i in movable]), rest
        for i in movable:
            addition = min(most - counts[i], max(1, remaining * portions[i] // whole), rest)
            counts[i] = counts[i] + addition
            rest = rest - addition
    return np.array([most] + counts)


def uneven_parts(own_key, number_of, total, reach, slope):
    if number_of == 2:
        one = jax.random.randint(own_key, (), max(1, total - reach), min(reach, total - 1) + 1)
        return jnp.stack([one, total - one])
    lengths = jnp.asarray(length_profile(number_of, total, reach, slope), jnp.int32)
    twos = (number_of - 1) // 2
    giver, sink = lengths[1:1 + 2 * twos:2], lengths[2:2 + 2 * twos:2]
    slack = jnp.minimum(giver - 1, reach - sink)
    shifted = jax.random.randint(jax.random.fold_in(own_key, 1), (twos,), 0, 1 << 20) % (slack + 1)
    lengths = lengths.at[1:1 + 2 * twos:2].set(giver - shifted).at[2:2 + 2 * twos:2].set(sink + shifted)
    return lengths[jax.random.permutation(jax.random.fold_in(own_key, 2), number_of)]


def gaussian(key, shape, deviation, most, cuts=(), held_as=jnp.bfloat16):
    level = level_of(key, shape, cuts, -0.22, 0.18) if cuts else 1.0
    values = jax.random.normal(key, shape, jnp.float32) * deviation * level
    return jnp.minimum(jnp.maximum(values, -most), most).astype(held_as)


def heavy_noise(key, dims, scale, most, shards, heavy, held_as=jnp.bfloat16):
    values = scale * jax.random.normal(key, dims, jnp.float32)
    if shards:
        values = values * level_of(key, dims, shards, -0.22, 0.18)
    return jnp.clip(raised(values, jax.random.fold_in(key, 3), *heavy), -most, most).astype(held_as)


def setup_inputs(seed: int = 0) -> dict:
    splits = jax.random.split(jax.random.key(seed), 14)
    return {
        "query_input": draw_query_input(jax.random.fold_in(splits[13], 71), 0),
        "key_input": draw_key_input(jax.random.fold_in(splits[13], 71), 0),
        "value_input": gaussian(splits[2], (SEQ_LEN, HEADS * HEAD_DIM), 1.0, 6.0, ((0, 16), (1, 2))),
        "segment_ids": jnp.searchsorted(jnp.cumsum(uneven_parts(splits[3], DOCS, SEQ_LEN, SEQ_LEN // 8, 1)), jnp.arange(SEQ_LEN), side="right").astype(jnp.int32),
        "residual_in": draw_residual_in(jax.random.fold_in(splits[13], 71), 0),
        "out_weight": heavy_noise(splits[5], (HEADS * HEAD_DIM, D), (HEADS * HEAD_DIM) ** -0.5, 0.1875, ((0, 2),), (0, 1, 2, 2.0)),
        "norm_gain": jnp.clip(1.0 + 0.18 * jax.random.normal(splits[6], (D,), jnp.float32), 0.1, 1.9),
        "router": gaussian(splits[7], (D, EXPERTS), (D // 4) ** -0.5, 0.1875, ((1, 16),)),
        "modality": draw_modality(jax.random.fold_in(splits[13], 71), 0),
        "expert_in": draw_expert_in(jax.random.fold_in(splits[13], 71), 0),
        "gate_weight": gaussian(splits[10], (EXPERTS, D, FF), D ** -0.5, 0.09375, ((0, 16), (2, 2))),
        "up_weight": gaussian(splits[11], (EXPERTS, D, FF), D ** -0.5, 0.09375, ((0, 16), (2, 2))),
        "down_weight": heavy_noise(splits[12], (EXPERTS, FF, D), FF ** -0.5, 0.15625, ((0, 16), (1, 2)), (1, 2, 2, 2.0)),
    }


NEGATIVE = -1e+30
EPSILON = 1e-05

def attend_block(query_input, key_input, value_input, segment_ids, out_weight, start):
    key_width = SEQ_LEN // 8 + TOK
    key_start = jnp.maximum(start - SEQ_LEN // 8, 0).astype(jnp.int32)
    query_rows = lax.dynamic_slice_in_dim(query_input, start, TOK, 0).astype(jnp.float32).reshape(TOK, HEADS, HEAD_DIM)
    key_rows = lax.dynamic_slice_in_dim(key_input, key_start, key_width, 0).astype(jnp.float32).reshape(key_width, HEADS, HEAD_DIM)
    value_rows = lax.dynamic_slice_in_dim(value_input, key_start, key_width, 0).astype(jnp.float32).reshape(key_width, HEADS, HEAD_DIM)
    query_seg = lax.dynamic_slice_in_dim(segment_ids, start, TOK, 0)
    key_seg = lax.dynamic_slice_in_dim(segment_ids, key_start, key_width, 0)
    query_pos = start + jnp.arange(TOK, dtype=jnp.int32)
    key_pos = key_start + jnp.arange(key_width, dtype=jnp.int32)
    allowed = (query_seg[:, None] == key_seg[None, :]) & (key_pos[None, :] <= query_pos[:, None])
    scores = jnp.einsum('qhd,khd->hqk', query_rows, key_rows) * HEAD_DIM ** (-0.5)
    masked = jnp.where(allowed[None], scores, NEGATIVE)
    peak = lax.optimization_barrier(jnp.max(masked, axis=2, keepdims=True))
    weights = jnp.where(allowed[None], jnp.exp(masked - peak), 0.0)
    denominators = lax.optimization_barrier(jnp.sum(weights, axis=2))
    probabilities = lax.optimization_barrier(weights.astype(jnp.bfloat16)).astype(jnp.float32)
    numerators = jnp.einsum('hqk,khd->qhd', probabilities, value_rows)
    attended = (numerators / jnp.transpose(denominators)[:, :, None]).astype(jnp.bfloat16)
    group_width = HEADS * HEAD_DIM // N_EXP
    attended = attended.reshape(TOK, N_EXP, group_width).astype(jnp.float32)
    pieces = jnp.einsum('tng,ngd->tnd', attended, out_weight.astype(jnp.float32).reshape(N_EXP, group_width, D))
    pieces = lax.optimization_barrier(pieces.astype(jnp.bfloat16)).astype(jnp.float32)
    return lax.optimization_barrier(jnp.sum(pieces, axis=1))

def expert_apply(items):
    expert_rows, gate_part, up_part, down_part, router_column = items
    gate_sum = jnp.dot(expert_rows, gate_part, preferred_element_type=jnp.float32)
    up_sum = jnp.dot(expert_rows, up_part, preferred_element_type=jnp.float32)
    logits = jnp.dot(expert_rows, router_column, preferred_element_type=jnp.float32)
    hidden = (jax.nn.silu(gate_sum) * up_sum * jax.nn.sigmoid(logits)[:, None]).astype(jnp.bfloat16)
    row_count = expert_rows.shape[0]
    pieces = jnp.einsum('rng,ngd->rnd', hidden.astype(jnp.float32).reshape(row_count, N_EXP, FF_DEV), down_part.astype(jnp.float32).reshape(N_EXP, FF_DEV, D))
    pieces = lax.optimization_barrier(pieces.astype(jnp.bfloat16)).astype(jnp.float32)
    return lax.optimization_barrier(jnp.sum(pieces, axis=1)).astype(jnp.bfloat16)

def reference(query_input, key_input, value_input, segment_ids, residual_in, out_weight, norm_gain, router, modality, expert_in, gate_weight, up_weight, down_weight):
    starts = jnp.arange(N_SEQ, dtype=jnp.int32) * TOK

    def one_block(start):
        return attend_block(query_input, key_input, value_input, segment_ids, out_weight, start)
    attention = lax.map(one_block, starts).reshape(SEQ_LEN, D)
    residual = residual_in.astype(jnp.float32) + attention
    norm_scale = lax.rsqrt(lax.optimization_barrier(jnp.sum(residual * residual, axis=1, keepdims=True)) / D + EPSILON)
    normed = (residual * norm_scale * norm_gain).astype(jnp.bfloat16)
    picked = (modality * MODAL_EXPERTS + expert_in).astype(jnp.int32)
    block_picks = picked.reshape(N_SEQ, TOK)
    one_hot = (block_picks[:, :, None] == jnp.arange(EXPERTS, dtype=jnp.int32)[None, None, :]).astype(jnp.int32)
    running = (jnp.cumsum(one_hot, axis=1) - 1).astype(jnp.int32)
    rank_in_block = lax.optimization_barrier(jnp.sum(one_hot * running, axis=2)).astype(jnp.int32)
    slot_index = (jnp.arange(N_SEQ, dtype=jnp.int32)[:, None] * CAPACITY + rank_in_block).reshape(SEQ_LEN).astype(jnp.int32)
    expert_rows = jnp.zeros((EXPERTS, N_SEQ * CAPACITY, D), jnp.bfloat16).at[picked, slot_index].set(normed)
    expert_outputs = lax.map(expert_apply, (expert_rows, gate_weight, up_weight, down_weight, jnp.transpose(router)))
    routed = expert_outputs[picked, slot_index]
    return (residual + routed.astype(jnp.float32)).astype(jnp.bfloat16)
```

```python
import functools

import jax
import jax.numpy as jnp
from jax import lax
from jax.experimental import pallas as pl
from jax.experimental.pallas import tpu as pltpu
from jax.sharding import PartitionSpec as P

HEAD_DIM = 128
MODAL_EXPERTS = 16
CAPACITY = 7
NEGATIVE = -1e30
EPSILON = 1e-05
ROWS = 16
MIB = 1 << 20

F32 = jnp.float32
BF16 = jnp.bfloat16

ANY = pl.BlockSpec(memory_space=pl.ANY)
VMEM = pl.BlockSpec(memory_space=pltpu.VMEM)


def tiles(width, size):
    return [(start, min(size, width - start)) for start in range(0, width, size)]


def dot(left, right, dims=((1,), (0,))):
    return lax.dot_general(left, right, (dims, ((), ())), preferred_element_type=F32)


def shifted(value, axis, steps):
    count = lax.axis_size(axis)
    leading, last = max(0, -steps), min(count, count - steps)
    return lax.ppermute(value, axis, [(source, source + steps) for source in range(leading, last)])


def rotated(value, axis, steps):
    count = lax.axis_size(axis)
    return lax.ppermute(value, axis, [(source, (source + steps) % count) for source in range(count)])


def cost(flops, moved):
    return pl.CostEstimate(flops=int(flops), bytes_accessed=int(moved), transcendentals=0)


def kernel_call(body, ins, out_shape, specs=None, scratch=(), flops=0, moved=0, limit=16):
    specs = specs or [VMEM] * len(ins)
    outs = jax.tree.map(lambda _: VMEM, out_shape)
    return pl.pallas_call(
        body,
        in_specs=specs,
        out_specs=outs,
        out_shape=out_shape,
        scratch_shapes=list(scratch),
        cost_estimate=cost(flops, moved),
        compiler_params=pltpu.CompilerParams(vmem_limit_bytes=limit * MIB),
    )(*ins)


def struct(shape, dtype):
    return jax.ShapeDtypeStruct(shape, dtype)


def fetch_weights(out_weight, gate_weight, up_weight, feature_count):
    group = lax.axis_size("exp")
    head_rows = out_weight.shape[0]
    experts, _, hidden = gate_weight.shape

    def body(*refs):
        out_ref, gate_ref, up_ref = refs[:3]
        sems = refs[-1]
        me = lax.axis_index("exp")
        copies = []
        for k in range(group):
            ahead = lax.rem(me + k, group)
            behind = lax.rem(me + group - k, group)
            columns = pl.ds(pl.multiple_of(ahead * feature_count, 128), feature_count)
            rows = pl.ds(pl.multiple_of(behind * feature_count, 128), feature_count)
            out_to, gate_to, up_to = refs[3:6] if k == 0 else [ref.at[k - 1] for ref in refs[6:9]]
            copies.append((out_ref.at[:, columns], out_to))
            copies.append((gate_ref.at[:, rows, :], gate_to))
            copies.append((up_ref.at[:, rows, :], up_to))
        started = [
            pltpu.make_async_copy(source, target, sems.at[index])
            for index, (source, target) in enumerate(copies)
        ]
        for copy in started:
            copy.start()
        for copy in started:
            copy.wait()

    own = (
        (head_rows, feature_count),
        (experts, feature_count, hidden),
        (experts, feature_count, hidden),
    )
    shapes = [pltpu.VMEM(shape, BF16) for shape in own]
    shapes += [pltpu.VMEM((group - 1, *shape), BF16) for shape in own]
    return kernel_call(
        body,
        (out_weight, gate_weight, up_weight),
        tuple(shapes),
        specs=[ANY] * 3,
        scratch=[pltpu.SemaphoreType.DMA((3 * group,))],
        moved=2 * (out_weight.size + gate_weight.size + up_weight.size),
        limit=1,
    )


def attend(query, blocks, query_segments, out_slices, gain_row):
    group = lax.axis_size("exp")
    tokens, columns = query.shape
    features = out_slices.shape[2]
    count = len(blocks)

    def body(*refs):
        query_ref, block_refs = refs[0], refs[1 : 1 + count]
        segments_ref, out_ref, gain_ref = refs[1 + count : 4 + count]
        attended_ref, send_refs = refs[4 + count], refs[5 + count :]
        own = segments_ref[...]
        masks = []
        for index, block in enumerate(block_refs):
            theirs = block[2 * tokens : 2 * tokens + ROWS, :tokens].astype(F32)[0:1, :]
            mask = jnp.broadcast_to(own, (tokens, tokens)) == jnp.broadcast_to(
                theirs, (tokens, tokens)
            )
            if index == 0:
                key_pos = lax.broadcasted_iota(jnp.int32, (tokens, tokens), 1)
                query_pos = lax.broadcasted_iota(jnp.int32, (tokens, tokens), 0)
                mask = mask & (key_pos <= query_pos)
            masks.append(mask)
        for head in range(columns // HEAD_DIM):
            part = slice(head * HEAD_DIM, (head + 1) * HEAD_DIM)
            heads = query_ref[:, part]
            scores = [
                jnp.where(
                    mask,
                    dot(heads, block[:tokens, part], ((1,), (1,))) * HEAD_DIM ** (-0.5),
                    NEGATIVE,
                )
                for block, mask in zip(block_refs, masks)
            ]
            peak = functools.reduce(
                jnp.maximum, [jnp.max(score, axis=1, keepdims=True) for score in scores]
            )
            weights = [jnp.exp(score - peak) for score in scores]
            total = sum(jnp.sum(weight, axis=1, keepdims=True) for weight in weights)
            summed = sum(
                dot(weight.astype(BF16), block[tokens : 2 * tokens, part])
                for weight, block in zip(weights, block_refs)
            )
            attended_ref[:, part] = (summed / total).astype(BF16)
        high = gain_ref[...].astype(BF16)
        low = (gain_ref[...] - high.astype(F32)).astype(BF16)
        row = lax.broadcasted_iota(jnp.int32, (ROWS, features), 0)
        gains = jnp.where(row == 0, high.astype(F32), jnp.where(row == 1, low.astype(F32), 0.0))
        for k, send in enumerate(send_refs):
            for start, width in tiles(features, 512):
                send[:tokens, start : start + width] = dot(
                    attended_ref[...], out_ref[k, :, start : start + width]
                ).astype(BF16)
            send[tokens : tokens + ROWS, :] = gains.astype(BF16)

    shapes = [struct((tokens, columns), BF16)]
    shapes += [struct((tokens + ROWS, features), BF16)] * (group - 1)
    return kernel_call(
        body,
        (query, *blocks, query_segments, out_slices, gain_row),
        tuple(shapes),
        flops=2 * tokens * columns * features * (group - 1),
        moved=2 * columns * features * (group - 1),
    )


def project_own(attended, out_slices):
    tokens, columns = attended.shape
    features = out_slices.shape[1]

    def body(attended_ref, out_ref, own_ref):
        for start, width in tiles(features, 512):
            own_ref[:, start : start + width] = dot(
                attended_ref[...], out_ref[:, start : start + width]
            ).astype(BF16)

    return kernel_call(
        body,
        (attended, out_slices),
        struct((tokens, features), BF16),
        flops=2 * tokens * columns * features,
        moved=2 * columns * features,
    )


def placement(picked, slots, devices, experts):
    tokens = picked.shape[1]
    expert = lax.broadcasted_iota(jnp.int32, (devices * experts, tokens), 0)
    chosen = expert == picked
    earlier = lax.broadcasted_iota(jnp.int32, (tokens, tokens), 0) < lax.broadcasted_iota(
        jnp.int32, (tokens, tokens), 1
    )
    before = dot(chosen.astype(F32).astype(BF16), earlier.astype(F32).astype(BF16))
    rank = jnp.sum(jnp.where(chosen, before, 0.0), axis=0, keepdims=True).astype(jnp.int32)
    target = lax.div(picked, jnp.full_like(picked, experts))
    local = picked - target * experts
    place = target * slots + local * CAPACITY + rank
    row = lax.broadcasted_iota(jnp.int32, (devices * slots, tokens), 0)
    return (row == place).astype(F32).astype(BF16)


def dispatch(own, received, residual_in, gain_row, modality, expert_in, slots, experts):
    devices = lax.axis_size("seq")
    tokens, features = own.shape
    count = len(received)

    def body(*refs):
        own_ref, received_refs = refs[0], refs[1 : 1 + count]
        residual_ref, gain_ref, modality_ref, expert_ref = refs[1 + count : 5 + count]
        total_ref, outgoing_ref = refs[5 + count :]
        picked = modality_ref[...] * MODAL_EXPERTS + expert_ref[...]
        places = placement(picked, slots, devices, experts)
        for start, width in tiles(features, 512):
            part = slice(start, start + width)
            attention = own_ref[:, part].astype(F32)
            for received_ref in received_refs:
                attention = attention + received_ref[:tokens, part].astype(F32)
            residual = residual_ref[:, part].astype(F32) + attention
            total_ref[:, part] = residual
            scaled = (residual * gain_ref[:, part]).astype(BF16)
            outgoing_ref[:, part] = dot(places, scaled).astype(BF16)

    return kernel_call(
        body,
        (own, *received, residual_in, gain_row, modality, expert_in),
        (struct((tokens, features), F32), struct((devices * slots, features), BF16)),
    )


def selection(expert, devices, slots, transpose):
    many, all_rows = devices * CAPACITY, devices * slots
    shape = (all_rows, many) if transpose else (many, all_rows)
    packed = lax.broadcasted_iota(jnp.int32, shape, 1 if transpose else 0)
    arrived = lax.broadcasted_iota(jnp.int32, shape, 0 if transpose else 1)
    shift = slots.bit_length() - 1
    source = arrived >> shift
    within = (arrived & (slots - 1)) - expert * CAPACITY
    hit = (within >= 0) & (within < CAPACITY) & (packed == source * CAPACITY + within)
    return hit.astype(F32).astype(BF16)


def take_rows(arrived_ref, rows_ref, expert, devices, slots):
    select = selection(expert, devices, slots, False)
    for start, width in tiles(rows_ref.shape[1], 512):
        part = slice(start, start + width)
        rows_ref[:, part] = dot(select, arrived_ref[:, part]).astype(BF16)


def row_statistics(rows_ref, gain, router_row):
    squares = logits = None
    for start, width in tiles(rows_ref.shape[1], 128):
        part = slice(start, start + width)
        row = rows_ref[:, part].astype(F32)
        plain = row * (1.0 / gain[:, part])
        product = row * router_row[:, part]
        squares = plain * plain if squares is None else squares + plain * plain
        logits = product if logits is None else logits + product
    return jnp.sum(squares, axis=1, keepdims=True), jnp.sum(logits, axis=1, keepdims=True)


def two_columns(first, second, rows):
    lane = lax.broadcasted_iota(jnp.int32, (rows, 128), 1)
    return jnp.where(lane == 0, first, jnp.where(lane == 1, second, 0.0))


def own_features(arrived, gate_slices, up_slices, gain_row, router_rows, slots):
    devices = lax.axis_size("seq")
    experts, features, hidden = gate_slices.shape
    many = devices * CAPACITY

    def body(arrived_ref, gate_ref, up_ref, gain_ref, router_ref, gates, ups, stats, rows_ref):
        me = lax.axis_index("exp")
        columns = pl.ds(pl.multiple_of(me * features, 128), features)
        for expert in range(experts):
            take_rows(arrived_ref, rows_ref, expert, devices, slots)
            router_row = router_ref[expert : expert + 1, columns].astype(F32)
            stats[expert] = two_columns(
                *row_statistics(rows_ref, gain_ref[...], router_row), many
            )
            for start, width in tiles(hidden, 256):
                part = slice(start, start + width)
                gates[expert, :, part] = dot(rows_ref[...], gate_ref[expert, :, part])
                ups[expert, :, part] = dot(rows_ref[...], up_ref[expert, :, part])

    return kernel_call(
        body,
        (arrived, gate_slices, up_slices, gain_row, router_rows),
        (
            pltpu.VMEM((experts, many, hidden), F32),
            pltpu.VMEM((experts, many, hidden), F32),
            pltpu.VMEM((experts, many, 128), F32),
        ),
        scratch=[pltpu.VMEM((many, features), BF16)],
        flops=4 * experts * many * features * hidden,
        moved=4 * experts * features * hidden,
        limit=8,
    )


def down_copies(down_ref, buffer, sems, target, features):
    experts, hidden, _ = down_ref.shape
    columns = pl.ds(pl.multiple_of(target * features, 128), features)
    copies = [
        pltpu.make_async_copy(down_ref.at[expert, :, columns], buffer.at[expert], sems.at[expert])
        for expert in range(experts)
    ]
    return copies


def expand_rows(hidden_ref, buffer, packed_ref, target_ref, devices, slots):
    experts, many, _ = hidden_ref.shape
    spread = [selection(expert, devices, slots, True) for expert in range(experts)]
    for start, width in tiles(target_ref.shape[1], 256):
        part = slice(start, start + width)
        laid = None
        for expert in range(experts):
            rows = dot(hidden_ref[expert], buffer[expert, :, part]).astype(BF16)
            placed = dot(spread[expert], rows)
            laid = placed if laid is None else laid + placed
        target_ref[:, part] = laid.astype(BF16)


def other_features(
    arrivals, gate_slices, up_slices, gains, router_rows, sums, down_weight, tokens, slots
):
    devices, group = lax.axis_size("seq"), lax.axis_size("exp")
    _, experts, features, hidden = gate_slices.shape
    many = devices * CAPACITY
    count = group - 1
    width_all = features * group

    def body(*refs):
        arrived_refs, refs = refs[:count], refs[count:]
        gain_refs, refs = refs[:count], refs[count:]
        gate_ref, up_ref, router_ref, gates, ups, stats, down_ref = refs[:7]
        hidden_ref, send_refs, refs = refs[7], refs[8 : 8 + count], refs[8 + count :]
        rows_ref, buffer, sems = refs
        me = lax.axis_index("exp")
        copies = [
            down_copies(
                down_ref, buffer.at[k], sems.at[k], lax.rem(me + k + 1, group), features
            )
            for k in range(count)
        ]
        for copy in [copy for some in copies for copy in some]:
            copy.start()
        for expert in range(experts):
            squares, logits = stats[expert][:, 0:1], stats[expert][:, 1:2]
            gate_sums = up_sums = None
            for k in range(count):
                behind = lax.rem(me + group - k - 1, group)
                columns = pl.ds(pl.multiple_of(behind * features, 128), features)
                take_rows(arrived_refs[k], rows_ref, expert, devices, slots)
                pair = gain_refs[k][tokens : tokens + ROWS, :].astype(F32)
                more_squares, more_logits = row_statistics(
                    rows_ref,
                    pair[0:1, :] + pair[1:2, :],
                    router_ref[expert : expert + 1, columns].astype(F32),
                )
                squares, logits = squares + more_squares, logits + more_logits
                if k < count - 1:
                    for start, width in tiles(hidden, 256):
                        part = slice(start, start + width)
                        gates[expert, :, part] += dot(
                            rows_ref[...], gate_ref[k, expert, :, part]
                        )
                        ups[expert, :, part] += dot(rows_ref[...], up_ref[k, expert, :, part])
            scale = lax.rsqrt(squares / width_all + EPSILON)
            router_gate = 1.0 / (1.0 + jnp.exp(-(logits * scale)))
            for start, width in tiles(hidden, 256):
                part = slice(start, start + width)
                gate = gates[expert, :, part] + dot(
                    rows_ref[...], gate_ref[count - 1, expert, :, part]
                )
                up = ups[expert, :, part] + dot(rows_ref[...], up_ref[count - 1, expert, :, part])
                gate, up = gate * scale, up * scale
                hidden_ref[expert, :, part] = (
                    gate / (1.0 + jnp.exp(-gate)) * up * router_gate
                ).astype(BF16)
        for k in range(count):
            for copy in copies[k]:
                copy.wait()
            expand_rows(hidden_ref, buffer.at[k], None, send_refs[k], devices, slots)

    shapes = [struct((experts, many, hidden), BF16)]
    shapes += [struct((devices * slots, features), BF16)] * count
    ins = (*arrivals, *gains, gate_slices, up_slices, router_rows, *sums, down_weight)
    return kernel_call(
        body,
        ins,
        tuple(shapes),
        specs=[VMEM] * (len(ins) - 1) + [ANY],
        scratch=[
            pltpu.VMEM((many, features), BF16),
            pltpu.VMEM((count, experts, hidden, features), BF16),
            pltpu.SemaphoreType.DMA((count, experts)),
        ],
        flops=6 * experts * many * features * hidden,
        moved=2 * experts * features * hidden,
        limit=22,
    )


def own_outputs(hidden_rows, down_weight, features, slots):
    devices = lax.axis_size("seq")
    experts, many, hidden = hidden_rows.shape

    def body(hidden_ref, down_ref, own_ref, buffer, sems):
        copies = down_copies(down_ref, buffer, sems, lax.axis_index("exp"), features)
        for copy in copies:
            copy.start()
        for copy in copies:
            copy.wait()
        expand_rows(hidden_ref, buffer, None, own_ref, devices, slots)

    return kernel_call(
        body,
        (hidden_rows, down_weight),
        struct((devices * slots, features), BF16),
        specs=[VMEM, ANY],
        scratch=[
            pltpu.VMEM((experts, hidden, features), BF16),
            pltpu.SemaphoreType.DMA((experts,)),
        ],
        flops=2 * experts * many * features * hidden,
        moved=2 * experts * features * hidden,
    )


def add_groups(own, received):
    def body(*refs):
        total = refs[0][...].astype(F32)
        for ref in refs[1:-1]:
            total = total + ref[...].astype(F32)
        refs[-1][...] = total.astype(BF16)

    return kernel_call(body, (own, *received), struct(own.shape, BF16))


def finish(residual, returned, modality, expert_in, slots, experts):
    devices = lax.axis_size("seq")
    tokens, features = residual.shape

    def body(residual_ref, returned_ref, modality_ref, expert_ref, out_ref):
        picked = modality_ref[...] * MODAL_EXPERTS + expert_ref[...]
        places = placement(picked, slots, devices, experts)
        for start, width in tiles(features, 512):
            part = slice(start, start + width)
            routed = dot(places, returned_ref[:, part], ((0,), (0,)))
            out_ref[:, part] = (residual_ref[:, part] + routed).astype(BF16)

    return kernel_call(
        body,
        (residual, returned, modality, expert_in),
        struct((tokens, features), BF16),
    )


def local(
    query_input,
    key_input,
    value_input,
    segment_ids,
    residual_in,
    out_weight,
    norm_gain,
    router,
    modality,
    expert_in,
    gate_weight,
    up_weight,
    down_weight,
):
    tokens, columns = query_input.shape
    features = residual_in.shape[1]
    devices, group = lax.axis_size("seq"), lax.axis_size("exp")
    experts = gate_weight.shape[0]
    slots = max(ROWS, 1 << (experts * CAPACITY - 1).bit_length())
    marks = segment_ids + 1
    gain_row = norm_gain.reshape(1, features)
    router_rows = router.T
    modality, expert_in = modality.reshape(1, tokens), expert_in.reshape(1, tokens)
    mark_rows = jnp.broadcast_to(
        jnp.tile(marks.astype(BF16), columns // tokens)[None, :], (ROWS, columns)
    )
    packed = jnp.concatenate([key_input, value_input, mark_rows], axis=0)
    blocks = [shifted(packed, "seq", step) for step in range(1, devices // 8 + 1)]
    out_own, gate_own, up_own, out_others, gate_others, up_others = [
        pltpu.with_memory_space_constraint(value, pltpu.VMEM)
        for value in fetch_weights(out_weight, gate_weight, up_weight, features)
    ]
    attended, *contributions = attend(
        query_input,
        [packed, *blocks],
        marks.astype(F32).reshape(tokens, 1),
        out_others,
        gain_row,
    )
    received = [rotated(value, "exp", k + 1) for k, value in enumerate(contributions)]
    own = project_own(attended, out_own)
    residual, outgoing = dispatch(
        own, received, residual_in, gain_row, modality, expert_in, slots, experts
    )

    def exchanged(value):
        value = value.reshape(devices, slots, features)
        value = lax.all_to_all(value, "seq", split_axis=0, concat_axis=0, tiled=True)
        return value.reshape(devices * slots, features)

    arrived = exchanged(outgoing)
    arrivals = [rotated(arrived, "exp", k) for k in range(1, group)]
    sums = own_features(arrived, gate_own, up_own, gain_row, router_rows, slots)
    hidden_rows, *partials = other_features(
        arrivals,
        gate_others,
        up_others,
        received,
        router_rows,
        sums,
        down_weight,
        tokens,
        slots,
    )
    others = [rotated(value, "exp", k + 1) for k, value in enumerate(partials)]
    own_part = own_outputs(hidden_rows, down_weight, features, slots)
    returned = exchanged(add_groups(own_part, others))
    return finish(residual, returned, modality, expert_in, slots, experts)


def solution(mesh):
    in_specs = (
        P("seq", "exp"),
        P("seq", "exp"),
        P("seq", "exp"),
        P("seq"),
        P("seq", "exp"),
        P("exp", None),
        P("exp"),
        P(None, "seq"),
        P("seq"),
        P("seq"),
        P("seq", None, "exp"),
        P("seq", None, "exp"),
        P("seq", "exp", None),
    )
    return jax.shard_map(
        local, mesh=mesh, in_specs=in_specs, out_specs=P("seq", "exp"), check_vma=False
    )
```

```python
import functools

import jax
import jax.numpy as jnp
from jax import lax
from jax.experimental import pallas as pl
from jax.experimental.pallas import tpu as pltpu
from jax.sharding import PartitionSpec as P

HEAD_DIM = 128
MODAL_EXPERTS = 16
CAPACITY = 7
NEGATIVE = -1e30
EPSILON = 1e-05
ROWS = 16
MIB = 1 << 20

F32 = jnp.float32
BF16 = jnp.bfloat16

ANY = pl.BlockSpec(memory_space=pl.ANY)
VMEM = pl.BlockSpec(memory_space=pltpu.VMEM)


def tiles(width, size):
    return [(start, min(size, width - start)) for start in range(0, width, size)]


def dot(left, right, dims=((1,), (0,))):
    return lax.dot_general(left, right, (dims, ((), ())), preferred_element_type=F32)


def shifted(value, axis, steps):
    count = lax.axis_size(axis)
    leading, last = max(0, -steps), min(count, count - steps)
    return lax.ppermute(value, axis, [(source, source + steps) for source in range(leading, last)])


def rotated(value, axis, steps):
    count = lax.axis_size(axis)
    return lax.ppermute(value, axis, [(source, (source + steps) % count) for source in range(count)])


def cost(flops, moved):
    return pl.CostEstimate(flops=int(flops), bytes_accessed=int(moved), transcendentals=0)


def kernel_call(body, ins, out_shape, specs=None, scratch=(), flops=0, moved=0, limit=16):
    specs = specs or [VMEM] * len(ins)
    outs = jax.tree.map(lambda _: VMEM, out_shape)
    return pl.pallas_call(
        body,
        in_specs=specs,
        out_specs=outs,
        out_shape=out_shape,
        scratch_shapes=list(scratch),
        cost_estimate=cost(flops, moved),
        compiler_params=pltpu.CompilerParams(vmem_limit_bytes=limit * MIB),
    )(*ins)


def struct(shape, dtype):
    return jax.ShapeDtypeStruct(shape, dtype)


def pack_keys(key_input, value_input, segment_row):
    tokens, columns = key_input.shape

    def body(key_ref, value_ref, segment_ref, packed_ref, row_ref, sems):
        pairs = (
            (segment_ref, row_ref),
            (key_ref, packed_ref.at[:tokens, :]),
            (value_ref, packed_ref.at[tokens : 2 * tokens, :]),
        )
        copies = [
            pltpu.make_async_copy(source, target, sems.at[index])
            for index, (source, target) in enumerate(pairs)
        ]
        for copy in copies:
            copy.start()
        copies[0].wait()
        marks = jnp.broadcast_to((row_ref[...] + 1).astype(F32), (ROWS, tokens)).astype(BF16)
        for start in range(0, columns, tokens):
            packed_ref[2 * tokens : 2 * tokens + ROWS, start : start + tokens] = marks
        for copy in copies[1:]:
            copy.wait()

    return kernel_call(
        body,
        [
            pltpu.with_memory_space_constraint(value, pltpu.HBM)
            for value in (key_input, value_input, segment_row)
        ],
        pltpu.VMEM((2 * tokens + ROWS, columns), BF16),
        specs=[ANY] * 3,
        scratch=[pltpu.VMEM((1, tokens), jnp.int32), pltpu.SemaphoreType.DMA((3,))],
        limit=4,
    )


def prepare(out_weight, gate_weight, up_weight, modality, expert_in, feature_count, layout):
    devices, group = lax.axis_size("seq"), lax.axis_size("exp")
    head_rows = out_weight.shape[0]
    experts, _, hidden = gate_weight.shape
    rows, _, spare, tile_count, _ = layout
    tokens = modality.shape[1]
    kinds = 2 if spare else 1
    many = devices * CAPACITY

    def body(*refs):
        out_ref, gate_ref, up_ref, modality_ref, expert_ref = refs[:5]
        out_own, out_others, places_ref, take_ref, spread_ref = refs[5:10]
        slices, sems = refs[10:-1], refs[-1]
        me = lax.axis_index("exp")
        copies = []
        for k in range(group):
            ahead = lax.rem(me + k, group)
            columns = pl.ds(pl.multiple_of(ahead * feature_count, 128), feature_count)
            copies.append((out_ref.at[:, columns], out_others.at[k - 1] if k else out_own))
        wanted = [(up_ref, 0)] + [(gate_ref, k) for k in range(group)]
        for which, (ref, k) in enumerate(wanted):
            behind = lax.rem(me + group - k, group)
            part = pl.ds(pl.multiple_of(behind * feature_count, 128), feature_count)
            for expert in range(experts):
                copies.append((ref.at[expert, part, :], slices[which * experts + expert]))
        started = [
            pltpu.make_async_copy(source, target, sems.at[index])
            for index, (source, target) in enumerate(copies)
        ]
        for copy in started:
            copy.start()
        picked = modality_ref[...] * MODAL_EXPERTS + expert_ref[...]
        main, last = placement(picked, layout, devices, experts)
        places_ref[0] = main
        for tile, value in enumerate(last):
            places_ref[1 + tile] = value
        for tile in range(tile_count):
            for kind in range(kinds):
                which = tile if kind else None
                for expert in range(experts):
                    start = (kind * experts + expert) * many
                    take_ref[tile, start : start + many, :] = selection(
                        expert, layout, devices, which
                    )
                spread_ref[tile, :, kind * experts * many : (kind + 1) * experts * many] = (
                    spreading(layout, experts, devices, which)
                )
        for copy in started:
            copy.wait()

    shapes = (
        pltpu.VMEM((head_rows, feature_count), BF16),
        pltpu.VMEM((group - 1, head_rows, feature_count), BF16),
        pltpu.VMEM((1 + (tile_count if spare else 0), devices * rows, tokens), BF16),
        pltpu.VMEM((tile_count, kinds * experts * many, devices * rows), BF16),
        pltpu.VMEM((tile_count, devices * rows, kinds * experts * many), BF16),
        *[pltpu.VMEM((feature_count, hidden), BF16)] * ((1 + group) * experts),
    )
    return kernel_call(
        body,
        (out_weight, gate_weight, up_weight, modality, expert_in),
        shapes,
        specs=[ANY] * 3 + [VMEM] * 2,
        scratch=[pltpu.SemaphoreType.DMA((group + (1 + group) * experts,))],
        moved=2 * (out_weight.size + gate_weight.size + up_weight.size),
        limit=4,
    )


def attend(query, blocks, out_slices, gain_row):
    group = lax.axis_size("exp")
    tokens, columns = query.shape
    features = out_slices.shape[2]
    count = len(blocks)

    def body(*refs):
        query_ref, block_refs = refs[0], refs[1 : 1 + count]
        out_ref, gain_ref = refs[1 + count : 3 + count]
        attended_ref, send_refs = refs[3 + count], refs[4 + count :]
        key_pos = lax.broadcasted_iota(jnp.int32, (tokens, tokens), 1)
        query_pos = lax.broadcasted_iota(jnp.int32, (tokens, tokens), 0)
        marks = block_refs[0][2 * tokens : 2 * tokens + ROWS, :tokens]
        own = dot(one_hot(key_pos == query_pos), marks, ((1,), (1,)))[:, 0:1]
        masks = []
        for index, block in enumerate(block_refs):
            theirs = block[2 * tokens : 2 * tokens + ROWS, :tokens].astype(F32)[0:1, :]
            mask = jnp.broadcast_to(own, (tokens, tokens)) == jnp.broadcast_to(
                theirs, (tokens, tokens)
            )
            if index == 0:
                mask = mask & (key_pos <= query_pos)
            masks.append(mask)
        for head in range(columns // HEAD_DIM):
            part = slice(head * HEAD_DIM, (head + 1) * HEAD_DIM)
            heads = query_ref[:, part]
            scores = [
                jnp.where(
                    mask,
                    dot(heads, block[:tokens, part], ((1,), (1,))) * HEAD_DIM ** (-0.5),
                    NEGATIVE,
                )
                for block, mask in zip(block_refs, masks)
            ]
            peak = functools.reduce(
                jnp.maximum, [jnp.max(score, axis=1, keepdims=True) for score in scores]
            )
            weights = [jnp.exp(score - peak) for score in scores]
            total = sum(jnp.sum(weight, axis=1, keepdims=True) for weight in weights)
            summed = sum(
                dot(weight.astype(BF16), block[tokens : 2 * tokens, part])
                for weight, block in zip(weights, block_refs)
            )
            attended_ref[:, part] = (summed / total).astype(BF16)
        high = gain_ref[...].astype(BF16)
        low = (gain_ref[...] - high.astype(F32)).astype(BF16)
        row = lax.broadcasted_iota(jnp.int32, (ROWS, features), 0)
        gains = jnp.where(row == 0, high.astype(F32), jnp.where(row == 1, low.astype(F32), 0.0))
        for k, send in enumerate(send_refs):
            for start, width in tiles(features, 512):
                send[:tokens, start : start + width] = dot(
                    attended_ref[...], out_ref[k, :, start : start + width]
                ).astype(BF16)
            send[tokens : tokens + ROWS, :] = gains.astype(BF16)

    shapes = [struct((tokens, columns), BF16)]
    shapes += [struct((tokens + ROWS, features), BF16)] * (group - 1)
    return kernel_call(
        body,
        (query, *blocks, out_slices, gain_row),
        tuple(shapes),
        flops=2 * tokens * columns * features * (group - 1),
        moved=2 * columns * features * (group - 1),
        limit=6,
    )


def project_own(attended, out_slices):
    tokens, columns = attended.shape
    features = out_slices.shape[1]

    def body(attended_ref, out_ref, own_ref):
        for start, width in tiles(features, 512):
            own_ref[:, start : start + width] = dot(
                attended_ref[...], out_ref[:, start : start + width]
            ).astype(BF16)

    return kernel_call(
        body,
        (attended, out_slices),
        struct((tokens, features), BF16),
        flops=2 * tokens * columns * features,
        moved=2 * columns * features,
        limit=4,
    )


def packing(features, experts):
    used = experts * CAPACITY
    rows = max(ROWS, 1 << (used - 1).bit_length())
    spare = rows - used
    if spare and used % spare == 0 and features % ((used // spare + 1) * 128) == 0:
        count = used // spare
        return rows, used, spare, count, features // (count + 1)
    return rows, used, 0, 1, features


def one_hot(hit):
    return hit.astype(F32).astype(BF16)


def placement(picked, layout, devices, experts):
    rows, used, spare, count, _ = layout
    tokens = picked.shape[1]
    expert = lax.broadcasted_iota(jnp.int32, (devices * experts, tokens), 0)
    chosen = expert == picked
    earlier = lax.broadcasted_iota(jnp.int32, (tokens, tokens), 0) < lax.broadcasted_iota(
        jnp.int32, (tokens, tokens), 1
    )
    before = dot(one_hot(chosen), one_hot(earlier))
    rank = jnp.sum(jnp.where(chosen, before, 0.0), axis=0, keepdims=True).astype(jnp.int32)
    target = lax.div(picked, jnp.full_like(picked, experts))
    slot = (picked - target * experts) * CAPACITY + rank
    row = lax.broadcasted_iota(jnp.int32, (devices * rows, tokens), 0)
    base = row - target * rows
    main = one_hot(base == slot)
    last = []
    for tile in range(count if spare else 0):
        within = slot - tile * spare
        last.append(one_hot((within >= 0) & (within < spare) & (base == used + within)))
    return main, last


def selection(expert, layout, devices, tile):
    rows, used, spare, _, _ = layout
    many, all_rows = devices * CAPACITY, devices * rows
    packed = lax.broadcasted_iota(jnp.int32, (many, all_rows), 0)
    arrived = lax.broadcasted_iota(jnp.int32, (many, all_rows), 1)
    source = arrived >> (rows.bit_length() - 1)
    slot = arrived & (rows - 1)
    if tile is None:
        fits = slot < used
    else:
        slot = slot - used
        fits = (slot >= 0) & (slot < spare)
        slot = slot + tile * spare
    within = slot - expert * CAPACITY
    hit = fits & (within >= 0) & (within < CAPACITY) & (packed == source * CAPACITY + within)
    return one_hot(hit)


def spreading(layout, experts, devices, tile):
    rows, used, spare, _, _ = layout
    many = devices * CAPACITY
    shape = (devices * rows, experts * many)
    row = lax.broadcasted_iota(jnp.int32, shape, 0)
    packed = lax.broadcasted_iota(jnp.int32, shape, 1)
    source = row >> (rows.bit_length() - 1)
    slot = row & (rows - 1)
    if tile is None:
        fits = slot < used
    else:
        slot = slot - used
        fits = (slot >= 0) & (slot < spare)
        slot = slot + tile * spare
    hit = None
    for expert in range(experts):
        within = slot - expert * CAPACITY
        here = (within >= 0) & (within < CAPACITY)
        here = here & (packed == expert * many + source * CAPACITY + within)
        hit = here if hit is None else hit | here
    return one_hot(fits & hit)


def tile_of(ref, layout, tile):
    rows = layout[0]
    value = ref[:, tile * rows : (tile + 1) * rows, :]
    return value.reshape(value.shape[0] * rows, value.shape[2])


def piece(layout, index):
    return slice(index * layout[4], (index + 1) * layout[4])


def dispatch(own, received, residual_in, gain_row, places, layout):
    devices = lax.axis_size("seq")
    tokens, features = own.shape
    count = len(received)
    rows, _, spare, tile_count, width = layout

    def body(*refs):
        own_ref, received_refs = refs[0], refs[1 : 1 + count]
        residual_ref, gain_ref, places_ref = refs[1 + count : 4 + count]
        total_ref, outgoing_ref = refs[4 + count :]

        def scaled(index):
            part = piece(layout, index)
            attention = own_ref[:, part].astype(F32)
            for received_ref in received_refs:
                attention = attention + received_ref[:tokens, part].astype(F32)
            residual = residual_ref[:, part].astype(F32) + attention
            total_ref[:, part] = residual
            return (residual * gain_ref[:, part]).astype(BF16)

        final = scaled(tile_count) if spare else None
        for tile in range(tile_count):
            laid = dot(places_ref[0], scaled(tile))
            if spare:
                laid = laid + dot(places_ref[1 + tile], final)
            outgoing_ref[:, tile * rows : (tile + 1) * rows, :] = laid.astype(BF16).reshape(
                devices, rows, width
            )

    return kernel_call(
        body,
        (own, *received, residual_in, gain_row, places),
        (
            struct((tokens, features), F32),
            struct((devices, tile_count * rows, width), BF16),
        ),
        limit=7,
    )


def take_rows(arrived_ref, take_ref, rows_ref, layout):
    _, _, spare, tile_count, _ = layout
    many = rows_ref.shape[0]
    final = None
    for tile in range(tile_count):
        taken = dot(take_ref[tile], tile_of(arrived_ref, layout, tile))
        rows_ref[:, piece(layout, tile)] = taken[:many].astype(BF16)
        if spare:
            final = taken[many:] if final is None else final + taken[many:]
    if spare:
        rows_ref[:, piece(layout, tile_count)] = final.astype(BF16)


def row_statistics(rows_ref, of_expert, gain, router_row):
    squares = logits = None
    inverse = 1.0 / gain
    for start, width in tiles(rows_ref.shape[1], 128):
        part = slice(start, start + width)
        row = rows_ref[of_expert, part].astype(F32)
        plain = row * inverse[:, part]
        product = row * router_row[:, part]
        squares = plain * plain if squares is None else squares + plain * plain
        logits = product if logits is None else logits + product
    return jnp.sum(squares, axis=1, keepdims=True), jnp.sum(logits, axis=1, keepdims=True)


def two_columns(first, second, rows):
    lane = lax.broadcasted_iota(jnp.int32, (rows, 128), 1)
    return jnp.where(lane == 0, first, jnp.where(lane == 1, second, 0.0))


def own_features(arrived, take, slices, gain_row, router_rows, layout):
    devices = lax.axis_size("seq")
    experts = len(slices) // 2
    features, hidden = slices[0].shape
    many = devices * CAPACITY

    def body(*refs):
        arrived_ref, take_ref, gain_ref, router_ref = refs[:4]
        up_refs, gate_refs = refs[4 : 4 + experts], refs[4 + experts : 4 + 2 * experts]
        gates, ups, stats, rows_ref = refs[4 + 2 * experts :]
        me = lax.axis_index("exp")
        columns = pl.ds(pl.multiple_of(me * features, 128), features)
        take_rows(arrived_ref, take_ref, rows_ref, layout)
        for expert in range(experts):
            of_expert = slice(expert * many, (expert + 1) * many)
            router_row = router_ref[expert : expert + 1, columns].astype(F32)
            stats[expert] = two_columns(
                *row_statistics(rows_ref, of_expert, gain_ref[...], router_row), many
            )
            for start, width in tiles(hidden, 256):
                part = slice(start, start + width)
                gates[expert, :, part] = dot(rows_ref[of_expert, :], gate_refs[expert][:, part])
                ups[expert, :, part] = dot(rows_ref[of_expert, :], up_refs[expert][:, part])

    return kernel_call(
        body,
        (arrived, take, gain_row, router_rows, *slices),
        (
            pltpu.VMEM((experts, many, hidden), F32),
            pltpu.VMEM((experts, many, hidden), F32),
            pltpu.VMEM((experts, many, 128), F32),
        ),
        scratch=[pltpu.VMEM((experts * many, features), BF16)],
        flops=4 * experts * many * features * hidden,
        moved=4 * experts * features * hidden,
        limit=8,
    )


def down_copies(down_ref, buffers, sems, first, target, features):
    columns = pl.ds(pl.multiple_of(target * features, 128), features)
    return [
        pltpu.make_async_copy(down_ref.at[expert, :, columns], buffer, sems.at[first + expert])
        for expert, buffer in enumerate(buffers)
    ]


def expand_rows(hidden_ref, down_refs, copies, spread_ref, laid_ref, target_ref, layout):
    rows, _, spare, tile_count, width = layout
    experts, many, _ = hidden_ref.shape
    devices = target_ref.shape[0]
    for expert in range(experts):
        copies[expert].wait()
        for index in range(laid_ref.shape[0]):
            laid_ref[index, expert * many : (expert + 1) * many, :] = dot(
                hidden_ref[expert], down_refs[expert][:, piece(layout, index)]
            ).astype(BF16)
    for tile in range(tile_count):
        laid = dot(spread_ref[tile, :, : experts * many], laid_ref[tile])
        if spare:
            laid = laid + dot(spread_ref[tile, :, experts * many :], laid_ref[tile_count])
        target_ref[:, tile * rows : (tile + 1) * rows, :] = laid.astype(BF16).reshape(
            devices, rows, width
        )


def laid_scratch(layout, experts, many):
    return pltpu.VMEM((layout[3] + (1 if layout[2] else 0), experts * many, layout[4]), BF16)


def other_features(
    arrivals,
    take,
    spread,
    gate_slices,
    up_weight,
    gains,
    router_rows,
    sums,
    down_weight,
    tokens,
    layout,
):
    devices, group = lax.axis_size("seq"), lax.axis_size("exp")
    experts = down_weight.shape[0]
    features, hidden = gate_slices[0].shape
    many = devices * CAPACITY
    count = group - 1
    width_all = features * group

    def body(*refs):
        arrived_refs, refs = refs[:count], refs[count:]
        gain_refs, refs = refs[:count], refs[count:]
        take_ref, spread_ref, router_ref, gates, ups, stats = refs[:6]
        gate_refs, refs = refs[6 : 6 + count * experts], refs[6 + count * experts :]
        up_from, down_ref, hidden_ref = refs[:3]
        send_refs = refs[3 : 3 + count]
        rows_ref, laid_ref, up_ref, buffer, up_sems, sems = refs[3 + count :]
        buffers = [buffer.at[index] for index in range(count * experts)]
        me = lax.axis_index("exp")
        up_copies = []
        for k in range(count):
            part = pl.ds(
                pl.multiple_of(lax.rem(me + group - k - 1, group) * features, 128), features
            )
            for expert in range(experts):
                index = k * experts + expert
                up_copies.append(
                    pltpu.make_async_copy(
                        up_from.at[expert, part, :], up_ref.at[index], up_sems.at[index]
                    )
                )
        for copy in up_copies:
            copy.start()
        copies = [
            down_copies(
                down_ref,
                buffers[k * experts : (k + 1) * experts],
                sems,
                k * experts,
                lax.rem(me + k + 1, group),
                features,
            )
            for k in range(count)
        ]
        for copy in [copy for some in copies for copy in some]:
            copy.start()
        statistics = [(stats[e][:, 0:1], stats[e][:, 1:2]) for e in range(experts)]
        for k in range(count):
            behind = lax.rem(me + group - k - 1, group)
            columns = pl.ds(pl.multiple_of(behind * features, 128), features)
            take_rows(arrived_refs[k], take_ref, rows_ref, layout)
            pair = gain_refs[k][tokens : tokens + ROWS, :].astype(F32)
            gain = pair[0:1, :] + pair[1:2, :]
            for expert in range(experts):
                of_expert = slice(expert * many, (expert + 1) * many)
                more = row_statistics(
                    rows_ref,
                    of_expert,
                    gain,
                    router_ref[expert : expert + 1, columns].astype(F32),
                )
                statistics[expert] = [a + b for a, b in zip(statistics[expert], more)]
                squares, logits = statistics[expert]
                scale = lax.rsqrt(squares / width_all + EPSILON)
                router_gate = 1.0 / (1.0 + jnp.exp(-(logits * scale)))
                for start, size in tiles(hidden, 256):
                    part = slice(start, start + size)
                    gate = gates[expert, :, part] + dot(
                        rows_ref[of_expert, :], gate_refs[k * experts + expert][:, part]
                    )
                    if k == count - 1:
                        gate = gate * scale
                        gate = gate / (1.0 + jnp.exp(-gate)) * (scale * router_gate)
                    gates[expert, :, part] = gate
            for expert in range(experts):
                of_expert = slice(expert * many, (expert + 1) * many)
                index = k * experts + expert
                up_copies[index].wait()
                for start, size in tiles(hidden, 256):
                    part = slice(start, start + size)
                    up = ups[expert, :, part] + dot(
                        rows_ref[of_expert, :], up_ref[index, :, part]
                    )
                    if k < count - 1:
                        ups[expert, :, part] = up
                    else:
                        hidden_ref[expert, :, part] = (gates[expert, :, part] * up).astype(BF16)
        for k in range(count):
            down_refs = buffers[k * experts : (k + 1) * experts]
            expand_rows(
                hidden_ref, down_refs, copies[k], spread_ref, laid_ref, send_refs[k], layout
            )

    rows, _, _, tile_count, width = layout
    ins = (*arrivals, *gains, take, spread, router_rows, *sums, *gate_slices)
    return kernel_call(
        body,
        (*ins, up_weight, down_weight),
        (
            pltpu.VMEM((experts, many, hidden), BF16),
            *[pltpu.VMEM((devices, tile_count * rows, width), BF16)] * count,
        ),
        specs=[VMEM] * len(ins) + [ANY] * 2,
        scratch=[
            pltpu.VMEM((experts * many, features), BF16),
            laid_scratch(layout, experts, many),
            pltpu.VMEM((count * experts, features, hidden), BF16),
            pltpu.VMEM((count * experts, hidden, features), BF16),
            pltpu.SemaphoreType.DMA((count * experts,)),
            pltpu.SemaphoreType.DMA((count * experts,)),
        ],
        flops=6 * experts * many * features * hidden,
        moved=6 * experts * features * hidden,
        limit=30,
    )


def own_outputs(hidden_rows, down_weight, spread, features, layout):
    devices = lax.axis_size("seq")
    rows, _, _, tile_count, width = layout
    experts, many, hidden = hidden_rows.shape

    def body(hidden_ref, spread_ref, down_ref, own_ref, laid_ref, buffer, sems):
        buffers = [buffer.at[expert] for expert in range(experts)]
        copies = down_copies(down_ref, buffers, sems, 0, lax.axis_index("exp"), features)
        for copy in copies:
            copy.start()
        expand_rows(hidden_ref, buffers, copies, spread_ref, laid_ref, own_ref, layout)

    return kernel_call(
        body,
        (hidden_rows, spread, down_weight),
        struct((devices, tile_count * rows, width), BF16),
        specs=[VMEM] * 2 + [ANY],
        scratch=[
            laid_scratch(layout, experts, many),
            pltpu.VMEM((experts, hidden, features), BF16),
            pltpu.SemaphoreType.DMA((experts,)),
        ],
        flops=2 * experts * many * features * hidden,
        moved=2 * experts * features * hidden,
        limit=20,
    )


def add_groups(own, received):
    def body(*refs):
        total = refs[0][...].astype(F32)
        for ref in refs[1:-1]:
            total = total + ref[...].astype(F32)
        refs[-1][...] = total.astype(BF16)

    return kernel_call(body, (own, *received), struct(own.shape, BF16), limit=8)


def finish(residual, returned, places, layout):
    tokens, features = residual.shape
    _, _, spare, tile_count, _ = layout

    def body(residual_ref, returned_ref, places_ref, out_ref):
        final = None
        for tile in range(tile_count):
            value = tile_of(returned_ref, layout, tile)
            part = piece(layout, tile)
            routed = dot(places_ref[0], value, ((0,), (0,)))
            out_ref[:, part] = (residual_ref[:, part] + routed).astype(BF16)
            if spare:
                more = dot(places_ref[1 + tile], value, ((0,), (0,)))
                final = more if final is None else final + more
        if spare:
            part = piece(layout, tile_count)
            out_ref[:, part] = (residual_ref[:, part] + final).astype(BF16)

    return kernel_call(
        body,
        (residual, returned, places),
        struct((tokens, features), BF16),
        limit=8,
    )


def local(
    query_input,
    key_input,
    value_input,
    segment_ids,
    residual_in,
    out_weight,
    norm_gain,
    router,
    modality,
    expert_in,
    gate_weight,
    up_weight,
    down_weight,
):
    tokens, columns = query_input.shape
    features = residual_in.shape[1]
    devices, group = lax.axis_size("seq"), lax.axis_size("exp")
    experts = gate_weight.shape[0]
    layout = packing(features, experts)
    gain_row = norm_gain.reshape(1, features)
    router_rows = router.T
    modality, expert_in = modality.reshape(1, tokens), expert_in.reshape(1, tokens)

    def held(value):
        return pltpu.with_memory_space_constraint(value, pltpu.VMEM)

    out_weight = pltpu.with_memory_space_constraint(out_weight, pltpu.HBM)
    gate_weight = pltpu.with_memory_space_constraint(gate_weight, pltpu.HBM)
    up_weight = pltpu.with_memory_space_constraint(up_weight, pltpu.HBM)
    down_weight = pltpu.with_memory_space_constraint(down_weight, pltpu.HBM)
    packed = pack_keys(key_input, value_input, segment_ids.reshape(1, tokens))
    blocks = [shifted(packed, "seq", step) for step in range(1, devices // 8 + 1)]
    prepared = prepare(
        out_weight, gate_weight, up_weight, modality, expert_in, features, layout
    )
    out_own, out_others, places, take, spread, *slices = [held(value) for value in prepared]
    attended, *contributions = attend(query_input, [packed, *blocks], out_others, gain_row)
    received = [rotated(value, "exp", k + 1) for k, value in enumerate(contributions)]
    own = project_own(attended, out_own)
    residual, outgoing = dispatch(own, received, residual_in, gain_row, places, layout)

    def exchanged(value):
        return lax.all_to_all(value, "seq", split_axis=0, concat_axis=0, tiled=True)

    arrived = exchanged(outgoing)
    arrivals = [rotated(arrived, "exp", k) for k in range(1, group)]
    sums = own_features(
        arrived, take, slices[: 2 * experts], gain_row, router_rows, layout
    )
    hidden_rows, *partials = other_features(
        arrivals,
        take,
        spread,
        slices[2 * experts :],
        up_weight,
        received,
        router_rows,
        [held(value) for value in sums],
        down_weight,
        tokens,
        layout,
    )
    hidden_rows = held(hidden_rows)
    others = [rotated(value, "exp", k + 1) for k, value in enumerate(partials)]
    own_part = own_outputs(hidden_rows, down_weight, spread, features, layout)
    returned = exchanged(add_groups(own_part, others))
    return finish(residual, returned, places, layout)


def solution(mesh):
    in_specs = (
        P("seq", "exp"),
        P("seq", "exp"),
        P("seq", "exp"),
        P("seq"),
        P("seq", "exp"),
        P("exp", None),
        P("exp"),
        P(None, "seq"),
        P("seq"),
        P("seq"),
        P("seq", None, "exp"),
        P("seq", None, "exp"),
        P("seq", "exp", None),
    )
    return jax.shard_map(
        local, mesh=mesh, in_specs=in_specs, out_specs=P("seq", "exp"), check_vma=False
    )
```

```python
import functools

import jax
import jax.numpy as jnp
from jax import lax
from jax.experimental import pallas as pl
from jax.experimental.pallas import tpu as pltpu
from jax.sharding import PartitionSpec as P

HEAD_DIM = 128
MODAL_EXPERTS = 16
CAPACITY = 7
NEGATIVE = -1e30
EPSILON = 1e-05
ROWS = 16
MIB = 1 << 20

F32 = jnp.float32
BF16 = jnp.bfloat16

ANY = pl.BlockSpec(memory_space=pl.ANY)
VMEM = pl.BlockSpec(memory_space=pltpu.VMEM)


def tiles(width, size):
    return [(start, min(size, width - start)) for start in range(0, width, size)]


def dot(left, right, dims=((1,), (0,))):
    return lax.dot_general(left, right, (dims, ((), ())), preferred_element_type=F32)


def shifted(value, axis, steps):
    count = lax.axis_size(axis)
    leading, last = max(0, -steps), min(count, count - steps)
    return lax.ppermute(value, axis, [(source, source + steps) for source in range(leading, last)])


def rotated(value, axis, steps):
    count = lax.axis_size(axis)
    return lax.ppermute(value, axis, [(source, (source + steps) % count) for source in range(count)])


def cost(flops, moved):
    return pl.CostEstimate(flops=int(flops), bytes_accessed=int(moved), transcendentals=0)


def kernel_call(body, ins, out_shape, specs=None, scratch=(), flops=0, moved=0, limit=16):
    specs = specs or [VMEM] * len(ins)
    outs = jax.tree.map(lambda _: VMEM, out_shape)
    return pl.pallas_call(
        body,
        in_specs=specs,
        out_specs=outs,
        out_shape=out_shape,
        scratch_shapes=list(scratch),
        cost_estimate=cost(flops, moved),
        compiler_params=pltpu.CompilerParams(vmem_limit_bytes=limit * MIB),
    )(*ins)


def struct(shape, dtype):
    return jax.ShapeDtypeStruct(shape, dtype)


def pack_keys(key_input, value_input, segment_row):
    tokens, columns = key_input.shape

    def body(key_ref, value_ref, segment_ref, packed_ref, row_ref, sems):
        pairs = (
            (segment_ref, row_ref),
            (key_ref, packed_ref.at[:tokens, :]),
            (value_ref, packed_ref.at[tokens : 2 * tokens, :]),
        )
        copies = [
            pltpu.make_async_copy(source, target, sems.at[index])
            for index, (source, target) in enumerate(pairs)
        ]
        for copy in copies:
            copy.start()
        copies[0].wait()
        marks = jnp.broadcast_to((row_ref[...] + 1).astype(F32), (ROWS, tokens)).astype(BF16)
        for start in range(0, columns, tokens):
            packed_ref[2 * tokens : 2 * tokens + ROWS, start : start + tokens] = marks
        for copy in copies[1:]:
            copy.wait()

    return kernel_call(
        body,
        [
            pltpu.with_memory_space_constraint(value, pltpu.HBM)
            for value in (key_input, value_input, segment_row)
        ],
        pltpu.VMEM((2 * tokens + ROWS, columns), BF16),
        specs=[ANY] * 3,
        scratch=[pltpu.VMEM((1, tokens), jnp.int32), pltpu.SemaphoreType.DMA((3,))],
        limit=4,
    )


def prepare(out_weight, gate_weight, up_weight, modality, expert_in, feature_count, layout):
    devices, group = lax.axis_size("seq"), lax.axis_size("exp")
    head_rows = out_weight.shape[0]
    experts, _, hidden = gate_weight.shape
    rows, _, spare, tile_count, _ = layout
    tokens = modality.shape[1]
    kinds = 2 if spare else 1
    many = devices * CAPACITY

    def body(*refs):
        out_ref, gate_ref, up_ref, modality_ref, expert_ref = refs[:5]
        out_own, out_others, places_ref, take_ref, spread_ref = refs[5:10]
        slices, sems = refs[10:-1], refs[-1]
        me = lax.axis_index("exp")
        copies = []
        for k in range(group):
            ahead = lax.rem(me + k, group)
            columns = pl.ds(pl.multiple_of(ahead * feature_count, 128), feature_count)
            copies.append((out_ref.at[:, columns], out_others.at[k - 1] if k else out_own))
        part = pl.ds(pl.multiple_of(me * feature_count, 128), feature_count)
        for which, ref in enumerate((up_ref, gate_ref)):
            for expert in range(experts):
                copies.append((ref.at[expert, part, :], slices[which * experts + expert]))
        started = [
            pltpu.make_async_copy(source, target, sems.at[index])
            for index, (source, target) in enumerate(copies)
        ]
        for copy in started:
            copy.start()
        picked = modality_ref[...] * MODAL_EXPERTS + expert_ref[...]
        main, last = placement(picked, layout, devices, experts)
        places_ref[0] = main
        for tile, value in enumerate(last):
            places_ref[1 + tile] = value
        for tile in range(tile_count):
            for kind in range(kinds):
                which = tile if kind else None
                for expert in range(experts):
                    start = (kind * experts + expert) * many
                    take_ref[tile, start : start + many, :] = selection(
                        expert, layout, devices, which
                    )
                spread_ref[tile, :, kind * experts * many : (kind + 1) * experts * many] = (
                    spreading(layout, experts, devices, which)
                )
        for copy in started:
            copy.wait()

    shapes = (
        pltpu.VMEM((head_rows, feature_count), BF16),
        pltpu.VMEM((group - 1, head_rows, feature_count), BF16),
        pltpu.VMEM((1 + (tile_count if spare else 0), devices * rows, tokens), BF16),
        pltpu.VMEM((tile_count, kinds * experts * many, devices * rows), BF16),
        pltpu.VMEM((tile_count, devices * rows, kinds * experts * many), BF16),
        *[pltpu.VMEM((feature_count, hidden), BF16)] * (2 * experts),
    )
    return kernel_call(
        body,
        (out_weight, gate_weight, up_weight, modality, expert_in),
        shapes,
        specs=[ANY] * 3 + [VMEM] * 2,
        scratch=[pltpu.SemaphoreType.DMA((group + 2 * experts,))],
        moved=2 * (out_weight.size + gate_weight.size + up_weight.size),
        limit=4,
    )


def attend(query, blocks, out_slices, gain_row):
    group = lax.axis_size("exp")
    tokens, columns = query.shape
    features = out_slices.shape[2]
    count = len(blocks)

    def body(*refs):
        query_ref, block_refs = refs[0], refs[1 : 1 + count]
        out_ref, gain_ref = refs[1 + count : 3 + count]
        attended_ref, send_refs = refs[3 + count], refs[4 + count :]
        key_pos = lax.broadcasted_iota(jnp.int32, (tokens, tokens), 1)
        query_pos = lax.broadcasted_iota(jnp.int32, (tokens, tokens), 0)
        marks = block_refs[0][2 * tokens : 2 * tokens + ROWS, :tokens]
        own = dot(one_hot(key_pos == query_pos), marks, ((1,), (1,)))[:, 0:1]
        masks = []
        for index, block in enumerate(block_refs):
            theirs = block[2 * tokens : 2 * tokens + ROWS, :tokens].astype(F32)[0:1, :]
            mask = jnp.broadcast_to(own, (tokens, tokens)) == jnp.broadcast_to(
                theirs, (tokens, tokens)
            )
            if index == 0:
                mask = mask & (key_pos <= query_pos)
            masks.append(mask)
        for head in range(columns // HEAD_DIM):
            part = slice(head * HEAD_DIM, (head + 1) * HEAD_DIM)
            heads = query_ref[:, part]
            scores = [
                jnp.where(
                    mask,
                    dot(heads, block[:tokens, part], ((1,), (1,))) * HEAD_DIM ** (-0.5),
                    NEGATIVE,
                )
                for block, mask in zip(block_refs, masks)
            ]
            peak = functools.reduce(
                jnp.maximum, [jnp.max(score, axis=1, keepdims=True) for score in scores]
            )
            weights = [jnp.exp(score - peak) for score in scores]
            total = sum(jnp.sum(weight, axis=1, keepdims=True) for weight in weights)
            summed = sum(
                dot(weight.astype(BF16), block[tokens : 2 * tokens, part])
                for weight, block in zip(weights, block_refs)
            )
            attended_ref[:, part] = (summed / total).astype(BF16)
        high = gain_ref[...].astype(BF16)
        low = (gain_ref[...] - high.astype(F32)).astype(BF16)
        row = lax.broadcasted_iota(jnp.int32, (ROWS, features), 0)
        gains = jnp.where(row == 0, high.astype(F32), jnp.where(row == 1, low.astype(F32), 0.0))
        for k, send in enumerate(send_refs):
            for start, width in tiles(features, 512):
                send[:tokens, start : start + width] = dot(
                    attended_ref[...], out_ref[k, :, start : start + width]
                ).astype(BF16)
            send[tokens : tokens + ROWS, :] = gains.astype(BF16)

    shapes = [struct((tokens, columns), BF16)]
    shapes += [struct((tokens + ROWS, features), BF16)] * (group - 1)
    return kernel_call(
        body,
        (query, *blocks, out_slices, gain_row),
        tuple(shapes),
        flops=2 * tokens * columns * features * (group - 1),
        moved=2 * columns * features * (group - 1),
        limit=6,
    )


def project_own(attended, out_slices):
    tokens, columns = attended.shape
    features = out_slices.shape[1]

    def body(attended_ref, out_ref, own_ref):
        for start, width in tiles(features, 512):
            own_ref[:, start : start + width] = dot(
                attended_ref[...], out_ref[:, start : start + width]
            ).astype(BF16)

    return kernel_call(
        body,
        (attended, out_slices),
        struct((tokens, features), BF16),
        flops=2 * tokens * columns * features,
        moved=2 * columns * features,
        limit=4,
    )


def packing(features, experts):
    used = experts * CAPACITY
    rows = max(ROWS, 1 << (used - 1).bit_length())
    spare = rows - used
    if spare and used % spare == 0 and features % ((used // spare + 1) * 128) == 0:
        count = used // spare
        return rows, used, spare, count, features // (count + 1)
    return rows, used, 0, 1, features


def one_hot(hit):
    return hit.astype(F32).astype(BF16)


def placement(picked, layout, devices, experts):
    rows, used, spare, count, _ = layout
    tokens = picked.shape[1]
    expert = lax.broadcasted_iota(jnp.int32, (devices * experts, tokens), 0)
    chosen = expert == picked
    earlier = lax.broadcasted_iota(jnp.int32, (tokens, tokens), 0) < lax.broadcasted_iota(
        jnp.int32, (tokens, tokens), 1
    )
    before = dot(one_hot(chosen), one_hot(earlier))
    rank = jnp.sum(jnp.where(chosen, before, 0.0), axis=0, keepdims=True).astype(jnp.int32)
    target = lax.div(picked, jnp.full_like(picked, experts))
    slot = (picked - target * experts) * CAPACITY + rank
    row = lax.broadcasted_iota(jnp.int32, (devices * rows, tokens), 0)
    base = row - target * rows
    main = one_hot(base == slot)
    last = []
    for tile in range(count if spare else 0):
        within = slot - tile * spare
        last.append(one_hot((within >= 0) & (within < spare) & (base == used + within)))
    return main, last


def selection(expert, layout, devices, tile):
    rows, used, spare, _, _ = layout
    many, all_rows = devices * CAPACITY, devices * rows
    packed = lax.broadcasted_iota(jnp.int32, (many, all_rows), 0)
    arrived = lax.broadcasted_iota(jnp.int32, (many, all_rows), 1)
    source = arrived >> (rows.bit_length() - 1)
    slot = arrived & (rows - 1)
    if tile is None:
        fits = slot < used
    else:
        slot = slot - used
        fits = (slot >= 0) & (slot < spare)
        slot = slot + tile * spare
    within = slot - expert * CAPACITY
    hit = fits & (within >= 0) & (within < CAPACITY) & (packed == source * CAPACITY + within)
    return one_hot(hit)


def spreading(layout, experts, devices, tile):
    rows, used, spare, _, _ = layout
    many = devices * CAPACITY
    shape = (devices * rows, experts * many)
    row = lax.broadcasted_iota(jnp.int32, shape, 0)
    packed = lax.broadcasted_iota(jnp.int32, shape, 1)
    source = row >> (rows.bit_length() - 1)
    slot = row & (rows - 1)
    if tile is None:
        fits = slot < used
    else:
        slot = slot - used
        fits = (slot >= 0) & (slot < spare)
        slot = slot + tile * spare
    hit = None
    for expert in range(experts):
        within = slot - expert * CAPACITY
        here = (within >= 0) & (within < CAPACITY)
        here = here & (packed == expert * many + source * CAPACITY + within)
        hit = here if hit is None else hit | here
    return one_hot(fits & hit)


def tile_of(ref, layout, tile):
    rows = layout[0]
    value = ref[:, tile * rows : (tile + 1) * rows, :]
    return value.reshape(value.shape[0] * rows, value.shape[2])


def piece(layout, index):
    return slice(index * layout[4], (index + 1) * layout[4])


def dispatch(own, received, residual_in, gain_row, places, layout):
    devices = lax.axis_size("seq")
    tokens, features = own.shape
    count = len(received)
    rows, _, spare, tile_count, width = layout

    def body(*refs):
        own_ref, received_refs = refs[0], refs[1 : 1 + count]
        residual_ref, gain_ref, places_ref = refs[1 + count : 4 + count]
        total_ref, outgoing_ref = refs[4 + count :]

        def scaled(index):
            part = piece(layout, index)
            attention = own_ref[:, part].astype(F32)
            for received_ref in received_refs:
                attention = attention + received_ref[:tokens, part].astype(F32)
            residual = residual_ref[:, part].astype(F32) + attention
            total_ref[:, part] = residual
            return (residual * gain_ref[:, part]).astype(BF16)

        final = scaled(tile_count) if spare else None
        for tile in range(tile_count):
            laid = dot(places_ref[0], scaled(tile))
            if spare:
                laid = laid + dot(places_ref[1 + tile], final)
            outgoing_ref[:, tile * rows : (tile + 1) * rows, :] = laid.astype(BF16).reshape(
                devices, rows, width
            )

    return kernel_call(
        body,
        (own, *received, residual_in, gain_row, places),
        (
            struct((tokens, features), F32),
            struct((devices, tile_count * rows, width), BF16),
        ),
        limit=7,
    )


def take_rows(arrived_ref, take_ref, rows_ref, layout):
    _, _, spare, tile_count, _ = layout
    many = rows_ref.shape[0]
    final = None
    for tile in range(tile_count):
        taken = dot(take_ref[tile], tile_of(arrived_ref, layout, tile))
        rows_ref[:, piece(layout, tile)] = taken[:many].astype(BF16)
        if spare:
            final = taken[many:] if final is None else final + taken[many:]
    if spare:
        rows_ref[:, piece(layout, tile_count)] = final.astype(BF16)


def row_statistics(rows_ref, of_expert, gain, router_row):
    squares = logits = None
    inverse = 1.0 / gain
    for start, width in tiles(rows_ref.shape[1], 128):
        part = slice(start, start + width)
        row = rows_ref[of_expert, part].astype(F32)
        plain = row * inverse[:, part]
        product = row * router_row[:, part]
        squares = plain * plain if squares is None else squares + plain * plain
        logits = product if logits is None else logits + product
    return jnp.sum(squares, axis=1, keepdims=True), jnp.sum(logits, axis=1, keepdims=True)


def two_columns(first, second, rows):
    lane = lax.broadcasted_iota(jnp.int32, (rows, 128), 1)
    return jnp.where(lane == 0, first, jnp.where(lane == 1, second, 0.0))


def own_features(arrived, take, slices, gain_row, router_rows, layout):
    devices = lax.axis_size("seq")
    experts = len(slices) // 2
    features, hidden = slices[0].shape
    many = devices * CAPACITY

    def body(*refs):
        arrived_ref, take_ref, gain_ref, router_ref = refs[:4]
        up_refs, gate_refs = refs[4 : 4 + experts], refs[4 + experts : 4 + 2 * experts]
        gates, ups, stats, rows_ref = refs[4 + 2 * experts :]
        me = lax.axis_index("exp")
        columns = pl.ds(pl.multiple_of(me * features, 128), features)
        take_rows(arrived_ref, take_ref, rows_ref, layout)
        for expert in range(experts):
            of_expert = slice(expert * many, (expert + 1) * many)
            router_row = router_ref[expert : expert + 1, columns].astype(F32)
            stats[expert] = two_columns(
                *row_statistics(rows_ref, of_expert, gain_ref[...], router_row), many
            )
            for start, width in tiles(hidden, 256):
                part = slice(start, start + width)
                gates[expert, :, part] = dot(rows_ref[of_expert, :], gate_refs[expert][:, part])
                ups[expert, :, part] = dot(rows_ref[of_expert, :], up_refs[expert][:, part])

    return kernel_call(
        body,
        (arrived, take, gain_row, router_rows, *slices),
        (
            pltpu.VMEM((experts, many, hidden), F32),
            pltpu.VMEM((experts, many, hidden), F32),
            pltpu.VMEM((experts, many, 128), F32),
        ),
        scratch=[pltpu.VMEM((experts * many, features), BF16)],
        flops=4 * experts * many * features * hidden,
        moved=4 * experts * features * hidden,
        limit=8,
    )


def down_copies(down_ref, buffers, sems, first, target, features):
    columns = pl.ds(pl.multiple_of(target * features, 128), features)
    return [
        pltpu.make_async_copy(down_ref.at[expert, :, columns], buffer, sems.at[first + expert])
        for expert, buffer in enumerate(buffers)
    ]


def expand_rows(hidden_ref, down_refs, copies, spread_ref, laid_ref, target_ref, layout):
    rows, _, spare, tile_count, width = layout
    experts, many, _ = hidden_ref.shape
    devices = target_ref.shape[0]
    for expert in range(experts):
        copies[expert].wait()
        for index in range(laid_ref.shape[0]):
            laid_ref[index, expert * many : (expert + 1) * many, :] = dot(
                hidden_ref[expert], down_refs[expert][:, piece(layout, index)]
            ).astype(BF16)
    for tile in range(tile_count):
        laid = dot(spread_ref[tile, :, : experts * many], laid_ref[tile])
        if spare:
            laid = laid + dot(spread_ref[tile, :, experts * many :], laid_ref[tile_count])
        target_ref[:, tile * rows : (tile + 1) * rows, :] = laid.astype(BF16).reshape(
            devices, rows, width
        )


def laid_scratch(layout, experts, many):
    return pltpu.VMEM((layout[3] + (1 if layout[2] else 0), experts * many, layout[4]), BF16)


def other_features(
    arrivals,
    take,
    spread,
    gate_weight,
    up_weight,
    gains,
    router_rows,
    sums,
    down_weight,
    tokens,
    layout,
):
    devices, group = lax.axis_size("seq"), lax.axis_size("exp")
    experts = down_weight.shape[0]
    features, hidden = gate_weight.shape[1] // group, gate_weight.shape[2]
    many = devices * CAPACITY
    count = group - 1
    width_all = features * group

    def body(*refs):
        arrived_refs, refs = refs[:count], refs[count:]
        gain_refs, refs = refs[:count], refs[count:]
        take_ref, spread_ref, router_ref, gates, ups, stats = refs[:6]
        gate_from, up_from, down_ref, hidden_ref = refs[6:10]
        send_refs = refs[10 : 10 + count]
        rows_ref, laid_ref, gate_ref, up_ref, buffer, gate_sems, up_sems, sems = refs[10 + count :]
        buffers = [buffer.at[index] for index in range(count * experts)]
        me = lax.axis_index("exp")
        gate_copies, up_copies = [], []
        for k in range(count):
            part = pl.ds(
                pl.multiple_of(lax.rem(me + group - k - 1, group) * features, 128), features
            )
            for expert in range(experts):
                index = k * experts + expert
                gate_copies.append(
                    pltpu.make_async_copy(
                        gate_from.at[expert, part, :], gate_ref.at[index], gate_sems.at[index]
                    )
                )
                up_copies.append(
                    pltpu.make_async_copy(
                        up_from.at[expert, part, :], up_ref.at[index], up_sems.at[index]
                    )
                )
        for copy in gate_copies + up_copies:
            copy.start()
        copies = [
            down_copies(
                down_ref,
                buffers[k * experts : (k + 1) * experts],
                sems,
                k * experts,
                lax.rem(me + k + 1, group),
                features,
            )
            for k in range(count)
        ]
        for copy in [copy for some in copies for copy in some]:
            copy.start()
        statistics = [(stats[e][:, 0:1], stats[e][:, 1:2]) for e in range(experts)]
        for k in range(count):
            behind = lax.rem(me + group - k - 1, group)
            columns = pl.ds(pl.multiple_of(behind * features, 128), features)
            take_rows(arrived_refs[k], take_ref, rows_ref, layout)
            pair = gain_refs[k][tokens : tokens + ROWS, :].astype(F32)
            gain = pair[0:1, :] + pair[1:2, :]
            for expert in range(experts):
                of_expert = slice(expert * many, (expert + 1) * many)
                more = row_statistics(
                    rows_ref,
                    of_expert,
                    gain,
                    router_ref[expert : expert + 1, columns].astype(F32),
                )
                statistics[expert] = [a + b for a, b in zip(statistics[expert], more)]
                squares, logits = statistics[expert]
                scale = lax.rsqrt(squares / width_all + EPSILON)
                router_gate = 1.0 / (1.0 + jnp.exp(-(logits * scale)))
                index = k * experts + expert
                gate_copies[index].wait()
                for start, size in tiles(hidden, 256):
                    part = slice(start, start + size)
                    gate = gates[expert, :, part] + dot(
                        rows_ref[of_expert, :], gate_ref[index, :, part]
                    )
                    if k == count - 1:
                        gate = gate * scale
                        gate = gate / (1.0 + jnp.exp(-gate)) * (scale * router_gate)
                    gates[expert, :, part] = gate
            for expert in range(experts):
                of_expert = slice(expert * many, (expert + 1) * many)
                index = k * experts + expert
                up_copies[index].wait()
                for start, size in tiles(hidden, 256):
                    part = slice(start, start + size)
                    up = ups[expert, :, part] + dot(
                        rows_ref[of_expert, :], up_ref[index, :, part]
                    )
                    if k < count - 1:
                        ups[expert, :, part] = up
                    else:
                        hidden_ref[expert, :, part] = (gates[expert, :, part] * up).astype(BF16)
        for k in range(count):
            down_refs = buffers[k * experts : (k + 1) * experts]
            expand_rows(
                hidden_ref, down_refs, copies[k], spread_ref, laid_ref, send_refs[k], layout
            )

    rows, _, _, tile_count, width = layout
    ins = (*arrivals, *gains, take, spread, router_rows, *sums)
    return kernel_call(
        body,
        (*ins, gate_weight, up_weight, down_weight),
        (
            pltpu.VMEM((experts, many, hidden), BF16),
            *[pltpu.VMEM((devices, tile_count * rows, width), BF16)] * count,
        ),
        specs=[VMEM] * len(ins) + [ANY] * 3,
        scratch=[
            pltpu.VMEM((experts * many, features), BF16),
            laid_scratch(layout, experts, many),
            pltpu.VMEM((count * experts, features, hidden), BF16),
            pltpu.VMEM((count * experts, features, hidden), BF16),
            pltpu.VMEM((count * experts, hidden, features), BF16),
            pltpu.SemaphoreType.DMA((count * experts,)),
            pltpu.SemaphoreType.DMA((count * experts,)),
            pltpu.SemaphoreType.DMA((count * experts,)),
        ],
        flops=6 * experts * many * features * hidden,
        moved=6 * experts * features * hidden,
        limit=42,
    )


def own_outputs(hidden_rows, down_weight, spread, features, layout):
    devices = lax.axis_size("seq")
    rows, _, _, tile_count, width = layout
    experts, many, hidden = hidden_rows.shape

    def body(hidden_ref, spread_ref, down_ref, own_ref, laid_ref, buffer, sems):
        buffers = [buffer.at[expert] for expert in range(experts)]
        copies = down_copies(down_ref, buffers, sems, 0, lax.axis_index("exp"), features)
        for copy in copies:
            copy.start()
        expand_rows(hidden_ref, buffers, copies, spread_ref, laid_ref, own_ref, layout)

    return kernel_call(
        body,
        (hidden_rows, spread, down_weight),
        struct((devices, tile_count * rows, width), BF16),
        specs=[VMEM] * 2 + [ANY],
        scratch=[
            laid_scratch(layout, experts, many),
            pltpu.VMEM((experts, hidden, features), BF16),
            pltpu.SemaphoreType.DMA((experts,)),
        ],
        flops=2 * experts * many * features * hidden,
        moved=2 * experts * features * hidden,
        limit=20,
    )


def add_groups(own, received):
    def body(*refs):
        total = refs[0][...].astype(F32)
        for ref in refs[1:-1]:
            total = total + ref[...].astype(F32)
        refs[-1][...] = total.astype(BF16)

    return kernel_call(body, (own, *received), struct(own.shape, BF16), limit=8)


def finish(residual, returned, places, layout):
    tokens, features = residual.shape
    _, _, spare, tile_count, _ = layout

    def body(residual_ref, returned_ref, places_ref, out_ref):
        final = None
        for tile in range(tile_count):
            value = tile_of(returned_ref, layout, tile)
            part = piece(layout, tile)
            routed = dot(places_ref[0], value, ((0,), (0,)))
            out_ref[:, part] = (residual_ref[:, part] + routed).astype(BF16)
            if spare:
                more = dot(places_ref[1 + tile], value, ((0,), (0,)))
                final = more if final is None else final + more
        if spare:
            part = piece(layout, tile_count)
            out_ref[:, part] = (residual_ref[:, part] + final).astype(BF16)

    return kernel_call(
        body,
        (residual, returned, places),
        struct((tokens, features), BF16),
        limit=8,
    )


def local(
    query_input,
    key_input,
    value_input,
    segment_ids,
    residual_in,
    out_weight,
    norm_gain,
    router,
    modality,
    expert_in,
    gate_weight,
    up_weight,
    down_weight,
):
    tokens, columns = query_input.shape
    features = residual_in.shape[1]
    devices, group = lax.axis_size("seq"), lax.axis_size("exp")
    experts = gate_weight.shape[0]
    layout = packing(features, experts)
    gain_row = norm_gain.reshape(1, features)
    router_rows = router.T
    modality, expert_in = modality.reshape(1, tokens), expert_in.reshape(1, tokens)

    def held(value):
        return pltpu.with_memory_space_constraint(value, pltpu.VMEM)

    out_weight = pltpu.with_memory_space_constraint(out_weight, pltpu.HBM)
    gate_weight = pltpu.with_memory_space_constraint(gate_weight, pltpu.HBM)
    up_weight = pltpu.with_memory_space_constraint(up_weight, pltpu.HBM)
    down_weight = pltpu.with_memory_space_constraint(down_weight, pltpu.HBM)
    packed = pack_keys(key_input, value_input, segment_ids.reshape(1, tokens))
    blocks = [shifted(packed, "seq", step) for step in range(1, devices // 8 + 1)]
    prepared = prepare(
        out_weight, gate_weight, up_weight, modality, expert_in, features, layout
    )
    out_own, out_others, places, take, spread, *slices = [held(value) for value in prepared]
    attended, *contributions = attend(query_input, [packed, *blocks], out_others, gain_row)
    received = [rotated(value, "exp", k + 1) for k, value in enumerate(contributions)]
    own = project_own(attended, out_own)
    residual, outgoing = dispatch(own, received, residual_in, gain_row, places, layout)

    def exchanged(value):
        return lax.all_to_all(value, "seq", split_axis=0, concat_axis=0, tiled=True)

    arrived = exchanged(outgoing)
    arrivals = [rotated(arrived, "exp", k) for k in range(1, group)]
    sums = own_features(
        arrived, take, slices, gain_row, router_rows, layout
    )
    hidden_rows, *partials = other_features(
        arrivals,
        take,
        spread,
        gate_weight,
        up_weight,
        received,
        router_rows,
        [held(value) for value in sums],
        down_weight,
        tokens,
        layout,
    )
    hidden_rows = held(hidden_rows)
    others = [rotated(value, "exp", k + 1) for k, value in enumerate(partials)]
    own_part = own_outputs(hidden_rows, down_weight, spread, features, layout)
    returned = exchanged(add_groups(own_part, others))
    return finish(residual, returned, places, layout)


def solution(mesh):
    in_specs = (
        P("seq", "exp"),
        P("seq", "exp"),
        P("seq", "exp"),
        P("seq"),
        P("seq", "exp"),
        P("exp", None),
        P("exp"),
        P(None, "seq"),
        P("seq"),
        P("seq"),
        P("seq", None, "exp"),
        P("seq", None, "exp"),
        P("seq", "exp", None),
    )
    return jax.shard_map(
        local, mesh=mesh, in_specs=in_specs, out_specs=P("seq", "exp"), check_vma=False
    )
```
